256 devices in a mesh: grp: 8 (over x, core), row: 32 (over z, y).
Axes of the slice: x: 4, y: 4, z: 8, core: 2. Of those that a mesh axis runs over, the one named last changes fastest.
Arguments:
- embeddings: float32 [131072, 4096], P(('grp', 'row')), may hold values from -225 to 225, as said below
- sketch: float32 [4096, 128], replicated, may hold values from -6 to 6
Outputs:
- row_basis: float32 [131072, 128], P(('grp', 'row'))
- column_factor: float32 [4096, 128], P(('grp', 'row'))
- first_factor: float32 [4096, 128], P(('grp', 'row'))
The draws below stay inside these ranges and needn't reach their ends.
Inputs may be any that keep to these rules, and one draw needn't show every extreme that they name: real-valued document embeddings.
All inputs are finite; a program needn't handle non-finite values.
Results may differ from the reference program's by a relative error of at most 0.000073.
Values sent between devices are 32-bit elements; how exact they have to be, the bound alone decides.
A program may use at most 64 MiB of HBM per device.

```python
import math
import jax
import jax.numpy as jnp
from jax import lax

D = 4096
K = 128
ROWS = 131072


def draw_embeddings(key, part):
    key = jax.random.fold_in(key, 7)
    first_key, second_key, third_key = jax.random.split(key, 3)
    base_values = jnp.clip(jax.random.normal(first_key, (ROWS, D), jnp.float32), -6.0, 6.0)
    row_scale = jnp.exp(jax.random.uniform(second_key, (ROWS, 1), jnp.float32) * jnp.log(10.0))
    ramp_scale = 1.0 + 2.0 * jnp.arange(ROWS, dtype=jnp.float32)[:, None] / ROWS
    column_scale = jnp.exp(jax.random.uniform(third_key, (1, D), jnp.float32) * jnp.log(10.0))
    return (base_values * row_scale * ramp_scale * column_scale / 8.0).astype(jnp.float32)


def noise(stream_key, dims, deviation, reach, kind=jnp.bfloat16):
    return jnp.clip(deviation * jax.random.normal(stream_key, dims, jnp.float32), -reach, reach).astype(kind)


def setup_inputs(seed: int = 0) -> dict:
    keys = jax.random.split(jax.random.key(seed), 3)
    return {
        "embeddings": draw_embeddings(jax.random.fold_in(keys[2], 71), 0),
        "sketch": noise(keys[1], (D, K), 1.0, 6.0, jnp.float32),
    }


def product(left, right):
    return jnp.dot(left.astype(jnp.float32), right.astype(jnp.float32), precision=lax.Precision.HIGHEST, preferred_element_type=jnp.float32)

def cholesky_basis(tall_block):
    gram_matrix = product(tall_block.T, tall_block)
    lower_factor = jnp.linalg.cholesky(gram_matrix)
    return jax.scipy.linalg.solve_triangular(lower_factor, tall_block.T, lower=True).T

def reference(embeddings, sketch):
    root_rows = math.sqrt(ROWS)
    first_image = product(embeddings, sketch)
    basis_one = cholesky_basis(first_image)
    back_product = product(embeddings.T, basis_one)
    second = product(embeddings, back_product)
    basis_two = cholesky_basis(second)
    column_factor = product(embeddings.T, basis_two) / root_rows
    return (basis_two * root_rows, column_factor, back_product / root_rows)
```

```python
import math

import jax
import jax.numpy as jnp
from jax import lax
from jax.experimental import pallas as pl
from jax.experimental.pallas import tpu as pltpu
from jax.sharding import PartitionSpec as P

MESH = pl.DeviceIdType.MESH
HIGHEST = lax.Precision.HIGHEST
F32, BF16 = jnp.float32, jnp.bfloat16
K = 128
NX, NY, NZ = 4, 4, 8
SLAB = 16
BLOCK = NY * NZ * SLAB
NBLOCK = 2 * NX


def split(value):
    high = value.astype(BF16)
    return high, (value - high.astype(F32)).astype(BF16)


def dot(left, right):
    return jnp.dot(left, right, preferred_element_type=F32)


def lane_broadcast(value, lane):
    return jnp.broadcast_to(value[:, lane : lane + 1], value.shape)


def row_broadcast(value, row):
    return jnp.broadcast_to(value[row : row + 1, :], value.shape)


def cholesky_inverse(tiles):
    lane = lax.broadcasted_iota(jnp.int32, (8, K), 1)
    sub = lax.broadcasted_iota(jnp.int32, (8, K), 0)
    tiles = list(tiles)
    for b in range(len(tiles)):
        cur = tiles[b]
        inside = (lane >= 8 * b) & (lane < 8 * b + 8)
        cols = [lane_broadcast(cur, 8 * b + k) for k in range(8)]
        low = {(i, k): row_broadcast(cols[k], i) for k in range(8) for i in range(k, 8)}
        rows = [
            jnp.where(inside, jnp.where(lane == 8 * b + i, 1.0, 0.0), row_broadcast(cur, i))
            for i in range(8)
        ]
        inv = []
        for k in range(8):
            inv.append(lax.rsqrt(low[k, k]))
            for i in range(k + 1, 8):
                low[i, k] = low[i, k] * inv[k]
            for i in range(k + 1, 8):
                for m in range(k + 1, i + 1):
                    low[i, m] = low[i, m] - low[i, k] * low[m, k]
        for k in range(8):
            rows[k] = rows[k] * inv[k]
            for i in range(k + 1, 8):
                rows[i] = rows[i] - low[i, k] * rows[k]
        for t in range(b + 1, len(tiles)):
            col = [lane_broadcast(tiles[t], 8 * b + k) for k in range(8)]
            acc = jnp.where(inside, 0.0, tiles[t])
            for k in range(8):
                col[k] = col[k] * inv[k]
                for m in range(k + 1, 8):
                    col[m] = col[m] - col[k] * low[m, k]
                acc = acc - col[k] * rows[k]
            tiles[t] = acc
        new = rows[0]
        for i in range(1, 8):
            new = jnp.where(sub == i, rows[i], new)
        tiles[b] = jnp.where(lane <= sub + 8 * b, new, 0.0)
    return tiles


def times_transposed(value, inverse):
    left_high, left_low = split(value)
    right_high, right_low = split(inverse.T)
    return dot(left_high, right_high) + (dot(left_high, right_low) + dot(left_low, right_high))


def kernel(
    x_hbm, s_hbm, basis_ref, column_ref, first_ref,
    x_in, s_in, x_high, x_low, s_pair, total, wide, tall,
    zfull,
    core_out, core_in, own, half, in1, part2, in2, part3, in3,
    gram, gram_in, gram_mid, gram_core, gram_z, gram_all, inverse,
    load_sem, core_send, core_recv, s1, r1, s2, r2, s3, r3,
    az_s, az_r, a2_s, a2_r, a1_s, a1_r, ac_s, ac_r,
    gx_s, gx_r, gc_s, gc_r, gz_s, gz_r, ga_s, ga_r,
):
    grp, row = lax.axis_index("grp"), lax.axis_index("row")
    x, core = grp // 2, grp % 2
    z, y = row // NY, row % NY
    other = 1 - core
    swap = core == 1
    first = jnp.where(swap, y, x)
    second = jnp.where(swap, x, y)
    place = first * 4 + second

    def device(px, pc, pz, py):
        return (px * 2 + pc, pz * NY + py)

    def along_first(step):
        at = lax.rem(first + step, 4)
        return at, device(jnp.where(swap, x, at), core, z, jnp.where(swap, at, y))

    def along_second(step):
        at = lax.rem(second + step, 4)
        return at, device(jnp.where(swap, at, x), core, z, jnp.where(swap, y, at))

    def along_z(step):
        at = lax.rem(z + step, NZ)
        return at, device(x, core, at, y)

    plane = [(i, j) for i in (2, 1, 3, 0) for j in (2, 1, 3, 0) if i or j]
    near = (2, 1, 3)
    ring = (4, 3, 5, 2, 6, 1, 7)

    def in_plane(step):
        px, py = lax.rem(x + step[0], 4), lax.rem(y + step[1], 4)
        return px * 4 + py, device(px, core, z, py)

    partner = device(x, other, z, y)

    def remote(src, dst, send, recv, to):
        return pltpu.make_async_remote_copy(
            src_ref=src, dst_ref=dst, send_sem=send, recv_sem=recv, device_id=to, device_id_type=MESH
        )

    barrier = pltpu.get_barrier_semaphore()
    peers = [partner] + [in_plane(s)[1] for s in plane] + [along_z(s)[1] for s in ring]
    for peer in peers:
        pl.semaphore_signal(barrier, inc=1, device_id=peer, device_id_type=MESH)

    loads = []
    for j in range(NBLOCK):
        cols = pl.ds(BLOCK * j, BLOCK)
        pair = (
            pltpu.make_async_copy(x_hbm.at[:, cols], x_in.at[j], load_sem.at[2 * j]),
            pltpu.make_async_copy(s_hbm.at[cols], s_in.at[j], load_sem.at[2 * j + 1]),
        )
        for copy in pair:
            copy.start()
        loads.append(pair)

    def start(copies):
        for copy in copies:
            copy.start()
        return copies

    def wait(copies):
        for copy in copies:
            copy.wait()

    def gram_start(g, block):
        gram[g] = dot_highest(block)
        return start([
            remote(gram.at[g, in_plane(s)[0]], gram_in.at[g, k], gx_s.at[g, k], gx_r.at[g, k], in_plane(s)[1])
            for k, s in enumerate(plane)
        ])

    def dot_highest(block):
        product = jnp.dot(block.T, block, precision=HIGHEST, preferred_element_type=F32)
        return product.reshape(16, 8, K)

    def gram_core_step(g, copies):
        wait(copies)
        tile = gram[g, x * 4 + y]
        for k in range(len(plane)):
            tile = tile + gram_in[g, k]
        gram_mid[g] = tile
        return start([remote(gram_mid.at[g], gram_core.at[g], gc_s.at[g], gc_r.at[g], partner)])

    def gram_z_step(g, copies):
        wait(copies)
        gram_z[g, z] = gram_mid[g] + gram_core[g]
        return start([
            remote(gram_z.at[g, z], gram_z.at[g, z], gz_s.at[g, k], gz_r.at[g, k], along_z(s)[1])
            for k, s in enumerate(ring)
        ])

    def gram_back_step(g, copies):
        wait(copies)
        tile = gram_z[g, 0]
        for k in range(1, NZ):
            tile = tile + gram_z[g, k]
        at = x * 4 + y
        gram_all[g, at] = tile
        return start([
            remote(gram_all.at[g, at], gram_all.at[g, at], ga_s.at[g, k], ga_r.at[g, k], in_plane(s)[1])
            for k, s in enumerate(plane)
        ])

    def gram_finish(g, copies):
        wait(copies)
        tiles = cholesky_inverse([gram_all[g, t] for t in range(16)])
        for t in range(16):
            inverse[g, pl.ds(8 * t, 8), :] = tiles[t]

    def transposed_block(j):
        part = dot(wide[...], x_high[j])
        part = part[0:K] + part[K : 2 * K] + dot(wide[0:K, :], x_low[j])
        return part.T.reshape(NZ, NY, SLAB, K)

    def prepare(block):
        high, low = split(block.T)
        wide[0:K, :] = high
        wide[K : 2 * K, :] = low

    def core_start(n):
        copies = []
        for px in range(NX):
            core_out[n, px] = transposed_block(px * 2 + other)
            copies += start([remote(core_out.at[n, px], core_in.at[n, px], core_send.at[n, px], core_recv.at[n, px], partner)])
        for px in range(NX):
            own[px] = transposed_block(px * 2 + core)
        return copies

    def first_step(n, copies):
        for px in range(NX):
            copies[px].wait()
            for py in range(NY):
                at = jnp.where(swap, py * 4 + px, px * 4 + py)
                half[n, at] = own[px, :, py] + core_in[n, px, :, py]
        return start([
            remote(half.at[n, pl.ds(along_first(s)[0] * 4, 4)], in1.at[n, k], s1.at[n, k], r1.at[n, k], along_first(s)[1])
            for k, s in enumerate(near)
        ])

    def second_step(n, copies):
        wait(copies)
        for i in range(4):
            part2[n, i] = (half[n, first * 4 + i] + in1[n, 0, i]) + (in1[n, 1, i] + in1[n, 2, i])
        return start([
            remote(part2.at[n, along_second(s)[0]], in2.at[n, k], s2.at[n, k], r2.at[n, k], along_second(s)[1])
            for k, s in enumerate(near)
        ])

    def z_step(n, copies):
        wait(copies)
        part3[n] = (part2[n, second] + in2[n, 0]) + (in2[n, 1] + in2[n, 2])
        return start([
            remote(part3.at[n, along_z(s)[0]], in3.at[n, k], s3.at[n, k], r3.at[n, k], along_z(s)[1])
            for k, s in enumerate(ring)
        ])

    def slab_of(n, copies):
        wait(copies)
        slab = part3[n, z]
        for k in range(len(ring)):
            slab = slab + in3[n, k]
        return slab

    total[...] = jnp.zeros_like(total)
    for j in range(NBLOCK):
        for copy in loads[j]:
            copy.wait()
        s_high, s_low = split(s_in[j])
        s_pair[j, :, 0:K] = s_high
        s_pair[j, :, K : 2 * K] = s_low
        high, low = split(x_in[j])
        x_high[j] = high
        x_low[j] = low
        part = dot(high, s_pair[j])
        total[...] += part[:, 0:K] + part[:, K : 2 * K] + dot(low, s_high)
    image = total[...]
    prepare(image)
    pl.semaphore_wait(barrier, len(peers))

    gram_copies = gram_start(0, image)
    copies = core_start(0)
    copies = first_step(0, copies)
    gram_copies = gram_core_step(0, gram_copies)
    gram_copies = gram_z_step(0, gram_copies)
    copies = second_step(0, copies)
    gram_copies = gram_back_step(0, gram_copies)
    copies = z_step(0, copies)
    slab = slab_of(0, copies)

    zfull[core, place, z] = slab
    copies = start([
        remote(zfull.at[core, place, z], zfull.at[core, place, z], az_s.at[k], az_r.at[k], along_z(s)[1])
        for k, s in enumerate(ring)
    ])
    wait(copies)
    copies = start([
        remote(zfull.at[core, place], zfull.at[core, place], a2_s.at[k], a2_r.at[k], along_second(s)[1])
        for k, s in enumerate(near)
    ])
    wait(copies)
    mine = pl.ds(first * 4, 4)
    copies = start([
        remote(zfull.at[core, mine], zfull.at[core, mine], a1_s.at[k], a1_r.at[k], along_first(s)[1])
        for k, s in enumerate(near)
    ])
    gram_finish(0, gram_copies)
    root_rows = math.sqrt(x_hbm.shape[0] * 256)
    first_ref[...] = times_transposed(slab, inverse[0]) / root_rows
    wait(copies)
    copies = start([remote(zfull.at[core], zfull.at[core], ac_s.at[0], ac_r.at[0], partner)])

    def image_of(half_core, px):
        for py in range(NY):
            at = jnp.where(half_core == 1, py * 4 + px, px * 4 + py)
            high, low = split(zfull[half_core, at])
            tall[px, :, py, :, 0:K] = high
            tall[px, :, py, :, K : 2 * K] = low
        right = tall[px].reshape(BLOCK, 2 * K)
        part = dot(x_high[px * 2 + half_core], right)
        return part[:, 0:K] + part[:, K : 2 * K] + dot(x_low[px * 2 + half_core], right[:, 0:K])

    total[...] = image_of(core, 0)
    for px in range(1, NX):
        total[...] += image_of(core, px)
    wait(copies)
    for px in range(NX):
        total[...] += image_of(other, px)
    total[...] = times_transposed(total[...], inverse[0])
    image = total[...]
    prepare(image)

    gram_copies = gram_start(1, image)
    copies = core_start(1)
    copies = first_step(1, copies)
    gram_copies = gram_core_step(1, gram_copies)
    gram_copies = gram_z_step(1, gram_copies)
    copies = second_step(1, copies)
    gram_copies = gram_back_step(1, gram_copies)
    copies = z_step(1, copies)
    gram_finish(1, gram_copies)
    basis_ref[...] = times_transposed(total[...], inverse[1]) * root_rows
    slab = slab_of(1, copies)
    column_ref[...] = times_transposed(slab, inverse[1]) / root_rows


def per_device(embeddings, sketch):
    rows = embeddings.shape[0]
    dma = pltpu.SemaphoreType.DMA
    vmem = pltpu.VMEM
    scratch = [
        vmem((NBLOCK, rows, BLOCK), F32),
        vmem((NBLOCK, BLOCK, K), F32),
        vmem((NBLOCK, rows, BLOCK), BF16),
        vmem((NBLOCK, rows, BLOCK), BF16),
        vmem((NBLOCK, BLOCK, 2 * K), BF16),
        vmem((rows, K), F32),
        vmem((2 * K, rows), BF16),
        vmem((NX, NZ, NY, SLAB, 2 * K), BF16),
        vmem((2, 16, NZ, SLAB, K), F32),
        vmem((2, NX, NZ, NY, SLAB, K), F32),
        vmem((2, NX, NZ, NY, SLAB, K), F32),
        vmem((NX, NZ, NY, SLAB, K), F32),
        vmem((2, 16, NZ, SLAB, K), F32),
        vmem((2, 3, 4, NZ, SLAB, K), F32),
        vmem((2, 4, NZ, SLAB, K), F32),
        vmem((2, 3, NZ, SLAB, K), F32),
        vmem((2, NZ, SLAB, K), F32),
        vmem((2, 7, SLAB, K), F32),
        vmem((2, 16, 8, K), F32),
        vmem((2, 15, 8, K), F32),
        vmem((2, 8, K), F32),
        vmem((2, 8, K), F32),
        vmem((2, NZ, 8, K), F32),
        vmem((2, 16, 8, K), F32),
        vmem((2, K, K), F32),
        dma((2 * NBLOCK,)),
        dma((2, NX)), dma((2, NX)),
        dma((2, 3)), dma((2, 3)),
        dma((2, 3)), dma((2, 3)),
        dma((2, 7)), dma((2, 7)),
        dma((7,)), dma((7,)),
        dma((3,)), dma((3,)),
        dma((3,)), dma((3,)),
        dma((1,)), dma((1,)),
        dma((2, 15)), dma((2, 15)),
        dma((2,)), dma((2,)),
        dma((2, 7)), dma((2, 7)),
        dma((2, 15)), dma((2, 15)),
    ]
    anywhere = pl.BlockSpec(memory_space=pl.ANY)
    return pl.pallas_call(
        kernel,
        name="subspace_iteration",
        out_shape=(
            jax.ShapeDtypeStruct((rows, K), F32),
            jax.ShapeDtypeStruct((SLAB, K), F32),
            jax.ShapeDtypeStruct((SLAB, K), F32),
        ),
        in_specs=[anywhere, anywhere],
        out_specs=[pl.BlockSpec(memory_space=pltpu.VMEM)] * 3,
        scratch_shapes=scratch,
        compiler_params=pltpu.CompilerParams(
            collective_id=0, has_side_effects=True, vmem_limit_bytes=48 * 2**20
        ),
        cost_estimate=pl.CostEstimate(
            flops=4 * 2 * rows * embeddings.shape[1] * K, bytes_accessed=11 * 2**20, transcendentals=0
        ),
    )(embeddings, sketch)


def solution(mesh):
    rows = P(("grp", "row"), None)
    return jax.shard_map(
        per_device, mesh=mesh, in_specs=(rows, P()), out_specs=(rows, rows, rows), check_vma=False
    )
```

```python
import math

import jax
import jax.numpy as jnp
from jax import lax
from jax.experimental import pallas as pl
from jax.experimental.pallas import tpu as pltpu
from jax.sharding import PartitionSpec as P

MESH = pl.DeviceIdType.MESH
HIGHEST = lax.Precision.HIGHEST
F32, BF16 = jnp.float32, jnp.bfloat16
K = 128
NX, NY, NZ = 4, 4, 8
SLAB = 16
BLOCK = NY * NZ * SLAB
NBLOCK = 2 * NX


def split(value):
    high = value.astype(BF16)
    return high, (value - high.astype(F32)).astype(BF16)


def dot(left, right):
    return jnp.dot(left, right, preferred_element_type=F32)


def lane_broadcast(value, lane):
    return jnp.broadcast_to(value[:, lane : lane + 1], value.shape)


def row_broadcast(value, row):
    return jnp.broadcast_to(value[row : row + 1, :], value.shape)


def eliminate(tiles, begin, end):
    lane = lax.broadcasted_iota(jnp.int32, (8, K), 1)
    sub = lax.broadcasted_iota(jnp.int32, (8, K), 0)
    tiles = list(tiles)
    for b in range(begin, end):
        cur = tiles[b]
        inside = (lane >= 8 * b) & (lane < 8 * b + 8)
        cols = [lane_broadcast(cur, 8 * b + k) for k in range(8)]
        low = {(i, k): row_broadcast(cols[k], i) for k in range(8) for i in range(k, 8)}
        rows = [
            jnp.where(inside, jnp.where(lane == 8 * b + i, 1.0, 0.0), row_broadcast(cur, i))
            for i in range(8)
        ]
        inv = []
        for k in range(8):
            inv.append(lax.rsqrt(low[k, k]))
            for i in range(k + 1, 8):
                low[i, k] = low[i, k] * inv[k]
            for i in range(k + 1, 8):
                for m in range(k + 1, i + 1):
                    low[i, m] = low[i, m] - low[i, k] * low[m, k]
        for k in range(8):
            rows[k] = rows[k] * inv[k]
            for i in range(k + 1, 8):
                rows[i] = rows[i] - low[i, k] * rows[k]
        for t in range(b + 1, len(tiles)):
            col = [lane_broadcast(tiles[t], 8 * b + k) for k in range(8)]
            acc = jnp.where(inside, 0.0, tiles[t])
            for k in range(8):
                col[k] = col[k] * inv[k]
                for m in range(k + 1, 8):
                    col[m] = col[m] - col[k] * low[m, k]
                acc = acc - col[k] * rows[k]
            tiles[t] = acc
        new = rows[0]
        for i in range(1, 8):
            new = jnp.where(sub == i, rows[i], new)
        tiles[b] = jnp.where(lane <= sub + 8 * b, new, 0.0)
    return tiles


def times_transposed(value, inverse):
    left_high, left_low = split(value)
    right_high, right_low = split(inverse.T)
    return dot(left_high, right_high) + (dot(left_high, right_low) + dot(left_low, right_high))


def kernel(
    x_hbm, s_hbm, basis_ref, column_ref, first_ref,
    x_in, s_in, x_high, x_low, s_pair, total, wide, tall,
    zfull,
    core_out, core_in, own, half, in1, part2, in2,
    gram, gram_in, gram_mid, gram_core, gram_z, gram_all, inverse,
    load_sem, core_send, core_recv, s1, r1, s2, r2,
    az_s, az_r, a1_s, a1_r, ac_s, ac_r,
    gx_s, gx_r, gc_s, gc_r, gz_s, gz_r, ga_s, ga_r,
):
    grp, row = lax.axis_index("grp"), lax.axis_index("row")
    x, core = grp // 2, grp % 2
    z, y = row // NY, row % NY
    other = 1 - core
    swap = core == 1
    first = jnp.where(swap, y, x)
    second = jnp.where(swap, x, y)

    def turn(at, step, size):
        return lax.rem(at + step, size)

    def device(px, pc, pz, py):
        return (px * 2 + pc, pz * NY + py)

    def by_axes(at_first, at_second, at_z):
        return device(jnp.where(swap, at_second, at_first), core, at_z, jnp.where(swap, at_first, at_second))

    near = (2, 1, 3)
    ring = (4, 3, 5, 2, 6, 1, 7)
    plane = [(i, j) for i in (2, 1, 3, 0) for j in (2, 1, 3, 0) if i or j]

    def in_plane(step):
        px, py = turn(x, step[0], NX), turn(y, step[1], NY)
        return px * 4 + py, device(px, core, z, py)

    partner = device(x, other, z, y)

    def remote(src, dst, send, recv, to):
        return pltpu.make_async_remote_copy(
            src_ref=src, dst_ref=dst, send_sem=send, recv_sem=recv, device_id=to, device_id_type=MESH
        )

    def arrived(ref, recv):
        remote(ref, ref, recv, recv, partner).wait_recv()

    def sent(ref, send):
        remote(ref, ref, send, send, partner).wait_send()

    loads = []
    for j in range(NBLOCK):
        cols = pl.ds(BLOCK * j, BLOCK)
        pair = (
            pltpu.make_async_copy(s_hbm.at[cols], s_in.at[j], load_sem.at[2 * j]),
            pltpu.make_async_copy(x_hbm.at[:, cols], x_in.at[j], load_sem.at[2 * j + 1]),
        )
        for copy in pair:
            copy.start()
        loads.append(pair)

    barrier = pltpu.get_barrier_semaphore()
    peers = [partner] + [in_plane(s)[1] for s in plane]
    peers += [by_axes(first, turn(second, i, 4), turn(z, k, NZ)) for i in range(4) for k in ring]
    for peer in peers:
        pl.semaphore_signal(barrier, inc=1, device_id=peer, device_id_type=MESH)

    def gram_start(g, block):
        product = jnp.dot(block.T, block, precision=HIGHEST, preferred_element_type=F32)
        gram[g] = product.reshape(16, 8, K)
        for k, s in enumerate(plane):
            at, to = in_plane(s)
            remote(gram.at[g, at], gram_in.at[g, k], gx_s.at[g], gx_r.at[g], to).start()

    def gram_core_step(g):
        arrived(gram_in.at[g], gx_r.at[g])
        tile = gram[g, x * 4 + y]
        for k in range(len(plane)):
            tile = tile + gram_in[g, k]
        gram_mid[g] = tile
        remote(gram_mid.at[g], gram_core.at[g], gc_s.at[g], gc_r.at[g], partner).start()

    def gram_z_step(g):
        arrived(gram_core.at[g], gc_r.at[g])
        gram_z[g, z] = gram_mid[g] + gram_core[g]
        for k in ring:
            to = by_axes(first, second, turn(z, k, NZ))
            remote(gram_z.at[g, z], gram_z.at[g, z], gz_s.at[g], gz_r.at[g], to).start()

    def gram_back_step(g):
        arrived(gram_z.at[g, pl.ds(0, 7)], gz_r.at[g])
        tile = gram_z[g, 0]
        for k in range(1, NZ):
            tile = tile + gram_z[g, k]
        at = x * 4 + y
        gram_all[g, at] = tile
        for s in plane:
            remote(gram_all.at[g, at], gram_all.at[g, at], ga_s.at[g], ga_r.at[g], in_plane(s)[1]).start()

    def gram_arrived(g):
        arrived(gram_all.at[g, pl.ds(0, 15)], ga_r.at[g])

    def factor(g, begin, end):
        source = gram_all if begin == 0 else inverse
        tiles = eliminate([source[g, t] for t in range(16)], begin, end)
        for t in range(16):
            inverse[g, t] = tiles[t]

    def inverse_of(g):
        return inverse[g].reshape(K, K)

    def transposed_block(j):
        part = dot(wide[...], x_high[j])
        part = part[0:K] + part[K : 2 * K] + dot(wide[0:K, :], x_low[j])
        return part.T.reshape(NZ, NY, SLAB, K)

    def prepare(block):
        high, low = split(block.T)
        wide[0:K, :] = high
        wide[K : 2 * K, :] = low

    def core_step(n):
        for px in range(NX):
            core_out[n, px] = transposed_block(px * 2 + other)
            remote(core_out.at[n, px], core_in.at[n, px], core_send.at[n, px], core_recv.at[n, px], partner).start()
        for px in range(NX):
            own[px] = transposed_block(px * 2 + core)

    def first_step(n):
        for px in range(NX):
            arrived(core_in.at[n, px], core_recv.at[n, px])
        for i, away in enumerate((2, 1, 3, 0)):
            at_second = turn(second, away, 4)
            for k, step in enumerate((2, 1, 3, 0)):
                at_first = turn(first, step, 4)
                px = jnp.where(swap, at_second, at_first)
                py = jnp.where(swap, at_first, at_second)
                half[n, i, k] = own[px, :, py] + core_in[n, px, :, py]
                if step:
                    to = by_axes(at_first, second, z)
                    remote(half.at[n, i, k], in1.at[n, i, k], s1.at[n], r1.at[n, i], to).start()

    def second_step(n, i):
        arrived(in1.at[n, i], r1.at[n, i])
        part2[n, i] = (half[n, i, 3] + in1[n, i, 0]) + (in1[n, i, 1] + in1[n, i, 2])
        at_second = turn(second, (2, 1, 3, 0)[i], 4)
        for k, step in enumerate(ring + (0,) if i < 3 else ring):
            at = turn(z, step, NZ)
            to = by_axes(first, at_second, at)
            remote(part2.at[n, i, at], in2.at[n, i * 8 + k], s2.at[n], r2.at[n], to).start()

    def slab_of(n):
        arrived(in2.at[n], r2.at[n])
        sums = [part2[n, 3, z]] + [in2[n, k] for k in range(31)]
        while len(sums) > 1:
            sums = [p + q for p, q in zip(sums[0::2], sums[1::2])]
        return sums[0]

    total[...] = jnp.zeros_like(total)
    for j in range(NBLOCK):
        for copy in loads[j]:
            copy.wait()
        s_high, s_low = split(s_in[j])
        s_pair[j, :, 0:K] = s_high
        s_pair[j, :, K : 2 * K] = s_low
        high, low = split(x_in[j])
        x_high[j] = high
        x_low[j] = low
        part = dot(high, s_pair[j])
        total[...] += part[:, 0:K] + part[:, K : 2 * K] + dot(low, s_high)
    image = total[...]
    prepare(image)
    pl.semaphore_wait(barrier, len(peers))

    gram_start(0, image)
    core_step(0)
    first_step(0)
    gram_core_step(0)
    gram_z_step(0)
    second_step(0, 0)
    second_step(0, 1)
    gram_back_step(0)
    second_step(0, 2)
    second_step(0, 3)
    slab = slab_of(0)

    zfull[core, first, second, z] = slab
    for away in (0, 1, 3, 2):
        for step in ring + (0,) if away else ring:
            to = by_axes(first, turn(second, away, 4), turn(z, step, NZ))
            mine = zfull.at[core, first, second, z]
            remote(mine, mine, az_s.at[0], az_r.at[away], to).start()
    gram_arrived(0)
    factor(0, 0, 7)
    for away in (0, 1, 3, 2):
        at_second = turn(second, 4 - away, 4)
        block = zfull.at[core, first, at_second]
        arrived(block if away else zfull.at[core, first, at_second, pl.ds(0, 7)], az_r.at[away])
        for step in near:
            to = by_axes(turn(first, step, 4), second, z)
            remote(block, block, a1_s.at[0], a1_r.at[away], to).start()
    factor(0, 7, 16)
    for away in (0, 1, 3, 2):
        block = zfull.at[core, :, turn(second, 4 - away, 4)]
        arrived(zfull.at[core, pl.ds(0, 3), 0], a1_r.at[away])
        remote(block, block, ac_s.at[0], ac_r.at[0], partner).start()
    root_rows = math.sqrt(x_hbm.shape[0] * 256)
    first_ref[...] = times_transposed(slab, inverse_of(0)) / root_rows

    def image_of(half_core, px):
        for py in range(NY):
            at_first = jnp.where(half_core == 1, py, px)
            at_second = jnp.where(half_core == 1, px, py)
            high, low = split(zfull[half_core, at_first, at_second])
            tall[px, :, py, :, 0:K] = high
            tall[px, :, py, :, K : 2 * K] = low
        right = tall[px].reshape(BLOCK, 2 * K)
        part = dot(x_high[px * 2 + half_core], right)
        return part[:, 0:K] + part[:, K : 2 * K] + dot(x_low[px * 2 + half_core], right[:, 0:K])

    total[...] = image_of(core, 0)
    for px in range(1, NX):
        total[...] += image_of(core, px)
    arrived(zfull.at[other], ac_r.at[0])
    for px in range(NX):
        total[...] += image_of(other, px)
    total[...] = times_transposed(total[...], inverse_of(0))
    image = total[...]
    prepare(image)

    gram_start(1, image)
    core_step(1)
    first_step(1)
    gram_core_step(1)
    gram_z_step(1)
    second_step(1, 0)
    second_step(1, 1)
    gram_back_step(1)
    second_step(1, 2)
    second_step(1, 3)
    gram_arrived(1)
    factor(1, 0, 16)
    basis_ref[...] = times_transposed(total[...], inverse_of(1)) * root_rows
    column_ref[...] = times_transposed(slab_of(1), inverse_of(1)) / root_rows

    for n in range(2):
        for px in range(NX):
            sent(core_out.at[n, px], core_send.at[n, px])
        sent(in1.at[n], s1.at[n])
        sent(in2.at[n], s2.at[n])
        sent(gram_in.at[n], gx_s.at[n])
        sent(gram_mid.at[n], gc_s.at[n])
        sent(gram_z.at[n, pl.ds(0, 7)], gz_s.at[n])
        sent(gram_all.at[n, pl.ds(0, 15)], ga_s.at[n])
    sent(in2.at[0], az_s.at[0])
    sent(in1.at[0], a1_s.at[0])
    sent(zfull.at[core], ac_s.at[0])


def per_device(embeddings, sketch):
    rows = embeddings.shape[0]
    dma = pltpu.SemaphoreType.DMA
    vmem = pltpu.VMEM
    scratch = [
        vmem((NBLOCK, rows, BLOCK), F32),
        vmem((NBLOCK, BLOCK, K), F32),
        vmem((NBLOCK, rows, BLOCK), BF16),
        vmem((NBLOCK, rows, BLOCK), BF16),
        vmem((NBLOCK, BLOCK, 2 * K), BF16),
        vmem((rows, K), F32),
        vmem((2 * K, rows), BF16),
        vmem((NX, NZ, NY, SLAB, 2 * K), BF16),
        vmem((2, 4, 4, NZ, SLAB, K), F32),
        vmem((2, NX, NZ, NY, SLAB, K), F32),
        vmem((2, NX, NZ, NY, SLAB, K), F32),
        vmem((NX, NZ, NY, SLAB, K), F32),
        vmem((2, 4, 4, NZ, SLAB, K), F32),
        vmem((2, 4, 3, NZ, SLAB, K), F32),
        vmem((2, 4, NZ, SLAB, K), F32),
        vmem((2, 31, SLAB, K), F32),
        vmem((2, 16, 8, K), F32),
        vmem((2, 15, 8, K), F32),
        vmem((2, 8, K), F32),
        vmem((2, 8, K), F32),
        vmem((2, NZ, 8, K), F32),
        vmem((2, 16, 8, K), F32),
        vmem((2, 16, 8, K), F32),
        dma((2 * NBLOCK,)),
        dma((2, NX)), dma((2, NX)),
        dma((2,)), dma((2, 4)),
        dma((2,)), dma((2,)),
        dma((1,)), dma((4,)),
        dma((1,)), dma((4,)),
        dma((1,)), dma((1,)),
        dma((2,)), dma((2,)),
        dma((2,)), dma((2,)),
        dma((2,)), dma((2,)),
        dma((2,)), dma((2,)),
    ]
    return pl.pallas_call(
        kernel,
        name="subspace_iteration",
        out_shape=(
            jax.ShapeDtypeStruct((rows, K), F32),
            jax.ShapeDtypeStruct((SLAB, K), F32),
            jax.ShapeDtypeStruct((SLAB, K), F32),
        ),
        in_specs=[pl.BlockSpec(memory_space=pltpu.HBM)] * 2,
        out_specs=[pl.BlockSpec(memory_space=pltpu.VMEM)] * 3,
        scratch_shapes=scratch,
        compiler_params=pltpu.CompilerParams(
            collective_id=0, has_side_effects=True, vmem_limit_bytes=52 * 2**20
        ),
        cost_estimate=pl.CostEstimate(
            flops=4 * 2 * rows * embeddings.shape[1] * K, bytes_accessed=11 * 2**20, transcendentals=0
        ),
    )(embeddings, sketch)


def solution(mesh):
    rows = P(("grp", "row"), None)
    return jax.shard_map(
        per_device, mesh=mesh, in_specs=(rows, P()), out_specs=(rows, rows, rows), check_vma=False
    )
```

```python
import math

import jax
import jax.numpy as jnp
from jax import lax
from jax.experimental import pallas as pl
from jax.experimental.pallas import tpu as pltpu
from jax.sharding import PartitionSpec as P

MESH = pl.DeviceIdType.MESH
HIGHEST = lax.Precision.HIGHEST
F32, BF16 = jnp.float32, jnp.bfloat16
K = 128
NX, NY, NZ = 4, 4, 8
SLAB = 16
BLOCK = NY * NZ * SLAB
NBLOCK = 2 * NX


def split(value):
    high = value.astype(BF16)
    return high, (value - high.astype(F32)).astype(BF16)


def dot(left, right):
    return jnp.dot(left, right, preferred_element_type=F32)


def lane_broadcast(value, lane):
    return jnp.broadcast_to(value[:, lane : lane + 1], value.shape)


def row_broadcast(value, row):
    return jnp.broadcast_to(value[row : row + 1, :], value.shape)


def unit_diagonal(tiles):
    lane = lax.broadcasted_iota(jnp.int32, (8, K), 1)
    sub = lax.broadcasted_iota(jnp.int32, (8, K), 0)
    diagonal = [jnp.where(lane == sub + 8 * t, tile, 0.0) for t, tile in enumerate(tiles)]
    total = diagonal
    while len(total) > 1:
        total = [p + q for p, q in zip(total[0::2], total[1::2])]
    across = jnp.broadcast_to(lax.rsqrt(jnp.sum(total[0], axis=0, keepdims=True)), (8, K))
    down = [lax.rsqrt(jnp.broadcast_to(jnp.sum(d, axis=1, keepdims=True), (8, K))) for d in diagonal]
    return [tile * d * across for tile, d in zip(tiles, down)], across


def eliminate(tiles):
    lane = lax.broadcasted_iota(jnp.int32, (8, K), 1)
    sub = lax.broadcasted_iota(jnp.int32, (8, K), 0)
    tiles = list(tiles)
    for b in range(len(tiles)):
        cur = tiles[b]
        inside = (lane >= 8 * b) & (lane < 8 * b + 8)
        cols = [lane_broadcast(cur, 8 * b + k) for k in range(8)]
        low = {(i, k): row_broadcast(cols[k], i) for k in range(8) for i in range(k, 8)}
        rows = [
            jnp.where(inside, jnp.where(lane == 8 * b + i, 1.0, 0.0), row_broadcast(cur, i))
            for i in range(8)
        ]
        inv = [None] * 8
        for k in range(0, 8, 2):
            p, q, r = low[k, k], low[k + 1, k], low[k + 1, k + 1]
            inv[k] = lax.rsqrt(p)
            inv[k + 1] = (p * inv[k]) * lax.rsqrt(p * r - q * q)
            low[k + 1, k] = q * inv[k]
            for i in range(k + 2, 8):
                low[i, k] = low[i, k] * inv[k]
                low[i, k + 1] = (low[i, k + 1] - low[i, k] * low[k + 1, k]) * inv[k + 1]
            for i in range(k + 2, 8):
                for m in range(k + 2, i + 1):
                    low[i, m] = (low[i, m] - low[i, k] * low[m, k]) - low[i, k + 1] * low[m, k + 1]
        for k in range(8):
            rows[k] = rows[k] * inv[k]
            for i in range(k + 1, 8):
                rows[i] = rows[i] - low[i, k] * rows[k]
        for t in range(b + 1, len(tiles)):
            col = [lane_broadcast(tiles[t], 8 * b + k) for k in range(8)]
            acc = jnp.where(inside, 0.0, tiles[t])
            for k in range(8):
                col[k] = col[k] * inv[k]
                for m in range(k + 1, 8):
                    col[m] = col[m] - col[k] * low[m, k]
                acc = acc - col[k] * rows[k]
            tiles[t] = acc
        new = rows[0]
        for i in range(1, 8):
            new = jnp.where(sub == i, rows[i], new)
        tiles[b] = jnp.where(lane <= sub + 8 * b, new, 0.0)
    return tiles


def times_transposed(value, inverse):
    left_high, left_low = split(value)
    right_high, right_low = split(inverse.T)
    return dot(left_high, right_high) + (dot(left_high, right_low) + dot(left_low, right_high))


def kernel(
    x_hbm, s_hbm, basis_ref, column_ref, first_ref,
    x_in, s_in, x_high, x_low, s_pair, total, wide, tall,
    zfull,
    core_out, core_in, own, half, in1, part2, in2,
    gram, gram_in, gram_mid, gram_core, gram_z, gram_all, inverse,
    load_sem, core_send, core_recv, s1, r1, s2, r2,
    az_s, az_r, a1_s, a1_r, ac_s, ac_r,
    gx_s, gx_r, gc_s, gc_r, gz_s, gz_r, ga_s, ga_r,
):
    grp, row = lax.axis_index("grp"), lax.axis_index("row")
    x, core = grp // 2, grp % 2
    z, y = row // NY, row % NY
    other = 1 - core
    swap = core == 1
    first = jnp.where(swap, y, x)
    second = jnp.where(swap, x, y)

    def turn(at, step, size):
        return lax.rem(at + step, size)

    def device(px, pc, pz, py):
        return (px * 2 + pc, pz * NY + py)

    def by_axes(at_first, at_second, at_z):
        return device(jnp.where(swap, at_second, at_first), core, at_z, jnp.where(swap, at_first, at_second))

    near = (2, 1, 3)
    far_first = near + (0,)
    ring = (4, 3, 5, 2, 6, 1, 7)
    plane = [(i, j) for i in (2, 1, 3, 0) for j in (2, 1, 3, 0) if i or j]

    def in_plane(step):
        px, py = turn(x, step[0], NX), turn(y, step[1], NY)
        return px * 4 + py, device(px, core, z, py)

    partner = device(x, other, z, y)

    def remote(src, dst, send, recv, to):
        return pltpu.make_async_remote_copy(
            src_ref=src, dst_ref=dst, send_sem=send, recv_sem=recv, device_id=to, device_id_type=MESH
        )

    def arrived(ref, recv):
        remote(ref, ref, recv, recv, partner).wait_recv()

    def sent(ref, send):
        remote(ref, ref, send, send, partner).wait_send()

    loads = []
    for j in range(NBLOCK):
        cols = pl.ds(BLOCK * j, BLOCK)
        pair = (
            pltpu.make_async_copy(s_hbm.at[cols], s_in.at[j], load_sem.at[2 * j]),
            pltpu.make_async_copy(x_hbm.at[:, cols], x_in.at[j], load_sem.at[2 * j + 1]),
        )
        for copy in pair:
            copy.start()
        loads.append(pair)

    barrier = pltpu.get_barrier_semaphore()
    peers = [partner] + [in_plane(s)[1] for s in plane]
    peers += [by_axes(first, turn(second, i, 4), turn(z, k, NZ)) for i in range(4) for k in ring]
    for peer in peers:
        pl.semaphore_signal(barrier, inc=1, device_id=peer, device_id_type=MESH)

    def gram_start(g, block):
        product = jnp.dot(block.T, block, precision=HIGHEST, preferred_element_type=F32)
        gram[g] = product.reshape(16, 8, K)
        for k, s in enumerate(plane):
            at, to = in_plane(s)
            remote(gram.at[g, at], gram_in.at[g, k], gx_s.at[g], gx_r.at[g], to).start()

    def gram_core_step(g):
        arrived(gram_in.at[g], gx_r.at[g])
        tile = gram[g, x * 4 + y]
        for k in range(len(plane)):
            tile = tile + gram_in[g, k]
        gram_mid[g] = tile
        remote(gram_mid.at[g], gram_core.at[g], gc_s.at[g], gc_r.at[g], partner).start()

    def gram_z_step(g):
        arrived(gram_core.at[g], gc_r.at[g])
        gram_z[g, z] = gram_mid[g] + gram_core[g]
        for k in ring:
            to = by_axes(first, second, turn(z, k, NZ))
            remote(gram_z.at[g, z], gram_z.at[g, z], gz_s.at[g], gz_r.at[g], to).start()

    def gram_back_step(g):
        arrived(gram_z.at[g, pl.ds(0, 7)], gz_r.at[g])
        tile = gram_z[g, 0]
        for k in range(1, NZ):
            tile = tile + gram_z[g, k]
        at = x * 4 + y
        gram_all[g, at] = tile
        for s in plane:
            remote(gram_all.at[g, at], gram_all.at[g, at], ga_s.at[g], ga_r.at[g], in_plane(s)[1]).start()

    def gram_arrived(g):
        arrived(gram_all.at[g, pl.ds(0, 15)], ga_r.at[g])

    def factor(g):
        tiles, across = unit_diagonal([gram_all[g, t] for t in range(16)])
        tiles = eliminate(tiles)
        for t in range(16):
            inverse[g, t] = tiles[t] * across

    def inverse_of(g):
        return inverse[g].reshape(K, K)

    def transposed_block(j):
        part = dot(wide[...], x_high[j])
        part = part[0:K] + part[K : 2 * K] + dot(wide[0:K, :], x_low[j])
        return part.T.reshape(NZ, NY, SLAB, K)

    def prepare(block):
        high, low = split(block.T)
        wide[0:K, :] = high
        wide[K : 2 * K, :] = low

    def core_step(n):
        for i, step in enumerate(far_first):
            core_out[n, i] = transposed_block(turn(x, step, NX) * 2 + other)
            remote(core_out.at[n, i], core_in.at[n, i], core_send.at[n, i], core_recv.at[n, i], partner).start()

    def first_step(n):
        for k, step in enumerate(far_first):
            own[k] = transposed_block(turn(x, step, NX) * 2 + core)
        for k in range(NX):
            arrived(core_in.at[n, k], core_recv.at[n, k])
        for i in range(4):
            for k, step in enumerate(far_first):
                xi = jnp.where(swap, i, k)
                py = turn(y, jnp.where(swap, step, far_first[i]), NY)
                half[n, i, k] = own[xi, :, py] + core_in[n, xi, :, py]
                if step:
                    to = by_axes(turn(first, step, 4), second, z)
                    remote(half.at[n, i, k], in1.at[n, i, k], s1.at[n], r1.at[n, i], to).start()

    def second_step(n, i):
        arrived(in1.at[n, i], r1.at[n, i])
        part2[n, i] = (half[n, i, 3] + in1[n, i, 0]) + (in1[n, i, 1] + in1[n, i, 2])
        at_second = turn(second, far_first[i], 4)
        for k, step in enumerate(ring + (0,) if i < 3 else ring):
            at = turn(z, step, NZ)
            to = by_axes(first, at_second, at)
            remote(part2.at[n, i, at], in2.at[n, i * 8 + k], s2.at[n], r2.at[n], to).start()

    def slab_of(n):
        arrived(in2.at[n], r2.at[n])
        sums = [part2[n, 3, z]] + [in2[n, k] for k in range(31)]
        while len(sums) > 1:
            sums = [p + q for p, q in zip(sums[0::2], sums[1::2])]
        return sums[0]

    total[...] = jnp.zeros_like(total)
    for j in range(NBLOCK):
        for copy in loads[j]:
            copy.wait()
        s_high, s_low = split(s_in[j])
        s_pair[j, :, 0:K] = s_high
        s_pair[j, :, K : 2 * K] = s_low
        high, low = split(x_in[j])
        x_high[j] = high
        x_low[j] = low
        part = dot(high, s_pair[j])
        total[...] += part[:, 0:K] + part[:, K : 2 * K] + dot(low, s_high)
    image = total[...]
    prepare(image)
    pl.semaphore_wait(barrier, len(peers))

    gram_start(0, image)
    core_step(0)
    first_step(0)
    gram_core_step(0)
    gram_z_step(0)
    second_step(0, 0)
    second_step(0, 1)
    gram_back_step(0)
    second_step(0, 2)
    second_step(0, 3)
    slab = slab_of(0)

    zfull[core, first, second, z] = slab
    for away in (0, 1, 3, 2):
        for step in ring + (0,) if away else ring:
            to = by_axes(first, turn(second, away, 4), turn(z, step, NZ))
            mine = zfull.at[core, first, second, z]
            remote(mine, mine, az_s.at[0], az_r.at[away], to).start()
    for away in (0, 1, 3, 2):
        at_second = turn(second, 4 - away, 4)
        block = zfull.at[core, first, at_second]
        arrived(block if away else zfull.at[core, first, at_second, pl.ds(0, 7)], az_r.at[away])
        for step in near:
            to = by_axes(turn(first, step, 4), second, z)
            remote(block, block, a1_s.at[0], a1_r.at[away], to).start()
    gram_arrived(0)
    factor(0)
    for away in (0, 1, 3, 2):
        block = zfull.at[core, :, turn(second, 4 - away, 4)]
        arrived(zfull.at[core, pl.ds(0, 3), 0], a1_r.at[away])
        remote(block, block, ac_s.at[0], ac_r.at[0], partner).start()
    root_rows = math.sqrt(x_hbm.shape[0] * 256)

    def image_of(half_core, px):
        for py in range(NY):
            at_first = jnp.where(half_core == 1, py, px)
            at_second = jnp.where(half_core == 1, px, py)
            high, low = split(zfull[half_core, at_first, at_second])
            tall[px, :, py, :, 0:K] = high
            tall[px, :, py, :, K : 2 * K] = low
        right = tall[px].reshape(BLOCK, 2 * K)
        part = dot(x_high[px * 2 + half_core], right)
        return part[:, 0:K] + part[:, K : 2 * K] + dot(x_low[px * 2 + half_core], right[:, 0:K])

    total[...] = image_of(core, 0)
    for px in range(1, NX):
        total[...] += image_of(core, px)
    arrived(zfull.at[other], ac_r.at[0])
    for px in range(NX):
        total[...] += image_of(other, px)
    total[...] = times_transposed(total[...], inverse_of(0))
    image = total[...]
    prepare(image)

    gram_start(1, image)
    core_step(1)
    first_step(1)
    gram_core_step(1)
    gram_z_step(1)
    second_step(1, 0)
    second_step(1, 1)
    gram_back_step(1)
    second_step(1, 2)
    second_step(1, 3)
    first_ref[...] = times_transposed(slab, inverse_of(0)) / root_rows
    gram_arrived(1)
    factor(1)
    basis_ref[...] = times_transposed(total[...], inverse_of(1)) * root_rows
    column_ref[...] = times_transposed(slab_of(1), inverse_of(1)) / root_rows

    for n in range(2):
        for px in range(NX):
            sent(core_out.at[n, px], core_send.at[n, px])
        sent(in1.at[n], s1.at[n])
        sent(in2.at[n], s2.at[n])
        sent(gram_in.at[n], gx_s.at[n])
        sent(gram_mid.at[n], gc_s.at[n])
        sent(gram_z.at[n, pl.ds(0, 7)], gz_s.at[n])
        sent(gram_all.at[n, pl.ds(0, 15)], ga_s.at[n])
    sent(in2.at[0], az_s.at[0])
    sent(in1.at[0], a1_s.at[0])
    sent(zfull.at[core], ac_s.at[0])


def hand_over(a, b, c, a_out, b_out, c_out, sem):
    copies = [
        pltpu.make_async_copy(src, dst, sem.at[k])
        for k, (src, dst) in enumerate(((a, a_out), (b, b_out), (c, c_out)))
    ]
    for copy in copies:
        copy.start()
    for copy in copies:
        copy.wait()


def per_device(embeddings, sketch):
    rows = embeddings.shape[0]
    dma = pltpu.SemaphoreType.DMA
    vmem = pltpu.VMEM
    scratch = [
        vmem((NBLOCK, rows, BLOCK), F32),
        vmem((NBLOCK, BLOCK, K), F32),
        vmem((NBLOCK, rows, BLOCK), BF16),
        vmem((NBLOCK, rows, BLOCK), BF16),
        vmem((NBLOCK, BLOCK, 2 * K), BF16),
        vmem((rows, K), F32),
        vmem((2 * K, rows), BF16),
        vmem((NX, NZ, NY, SLAB, 2 * K), BF16),
        vmem((2, 4, 4, NZ, SLAB, K), F32),
        vmem((2, NX, NZ, NY, SLAB, K), F32),
        vmem((2, NX, NZ, NY, SLAB, K), F32),
        vmem((NX, NZ, NY, SLAB, K), F32),
        vmem((2, 4, 4, NZ, SLAB, K), F32),
        vmem((2, 4, 3, NZ, SLAB, K), F32),
        vmem((2, 4, NZ, SLAB, K), F32),
        vmem((2, 31, SLAB, K), F32),
        vmem((2, 16, 8, K), F32),
        vmem((2, 15, 8, K), F32),
        vmem((2, 8, K), F32),
        vmem((2, 8, K), F32),
        vmem((2, NZ, 8, K), F32),
        vmem((2, 16, 8, K), F32),
        vmem((2, 16, 8, K), F32),
        dma((2 * NBLOCK,)),
        dma((2, NX)), dma((2, NX)),
        dma((2,)), dma((2, 4)),
        dma((2,)), dma((2,)),
        dma((1,)), dma((4,)),
        dma((1,)), dma((4,)),
        dma((1,)), dma((1,)),
        dma((2,)), dma((2,)),
        dma((2,)), dma((2,)),
        dma((2,)), dma((2,)),
        dma((2,)), dma((2,)),
    ]
    results = pl.pallas_call(
        kernel,
        name="subspace_iteration",
        out_shape=(
            jax.ShapeDtypeStruct((rows, K), F32),
            jax.ShapeDtypeStruct((SLAB, K), F32),
            jax.ShapeDtypeStruct((SLAB, K), F32),
        ),
        in_specs=[pl.BlockSpec(memory_space=pltpu.HBM)] * 2,
        out_specs=[pl.BlockSpec(memory_space=pltpu.VMEM)] * 3,
        scratch_shapes=scratch,
        compiler_params=pltpu.CompilerParams(
            collective_id=0, has_side_effects=True, vmem_limit_bytes=52 * 2**20
        ),
        cost_estimate=pl.CostEstimate(
            flops=4 * 2 * rows * embeddings.shape[1] * K, bytes_accessed=11 * 2**20, transcendentals=0
        ),
    )(embeddings, sketch)
    return pl.pallas_call(
        hand_over,
        name="hand_over",
        out_shape=tuple(jax.ShapeDtypeStruct(r.shape, r.dtype) for r in results),
        in_specs=[pl.BlockSpec(memory_space=pl.ANY)] * 3,
        out_specs=[pl.BlockSpec(memory_space=pl.ANY)] * 3,
        scratch_shapes=[dma((3,))],
        compiler_params=pltpu.CompilerParams(vmem_limit_bytes=2**20),
    )(*results)


def solution(mesh):
    rows = P(("grp", "row"), None)
    return jax.shard_map(
        per_device, mesh=mesh, in_specs=(rows, P()), out_specs=(rows, rows, rows), check_vma=False
    )
```

```python
import math

import jax
import jax.numpy as jnp
from jax import lax
from jax.experimental import pallas as pl
from jax.experimental.pallas import tpu as pltpu
from jax.sharding import PartitionSpec as P

MESH = pl.DeviceIdType.MESH
HIGHEST = lax.Precision.HIGHEST
F32, BF16 = jnp.float32, jnp.bfloat16
K = 128
NX, NY, NZ = 4, 4, 8
SLAB = 16
BLOCK = NY * NZ * SLAB
NBLOCK = 2 * NX


def split(value):
    high = value.astype(BF16)
    return high, (value - high.astype(F32)).astype(BF16)


def dot(left, right):
    return jnp.dot(left, right, preferred_element_type=F32)


def lane_broadcast(value, lane):
    return jnp.broadcast_to(value[:, lane : lane + 1], value.shape)


def row_broadcast(value, row):
    return jnp.broadcast_to(value[row : row + 1, :], value.shape)


def unit_diagonal(tiles):
    lane = lax.broadcasted_iota(jnp.int32, (8, K), 1)
    sub = lax.broadcasted_iota(jnp.int32, (8, K), 0)
    diagonal = [jnp.where(lane == sub + 8 * t, tile, 0.0) for t, tile in enumerate(tiles)]
    total = diagonal
    while len(total) > 1:
        total = [p + q for p, q in zip(total[0::2], total[1::2])]
    across = jnp.broadcast_to(lax.rsqrt(jnp.sum(total[0], axis=0, keepdims=True)), (8, K))
    down = [lax.rsqrt(jnp.broadcast_to(jnp.sum(d, axis=1, keepdims=True), (8, K))) for d in diagonal]
    return [tile * d * across for tile, d in zip(tiles, down)], across


def eliminate(tiles):
    lane = lax.broadcasted_iota(jnp.int32, (8, K), 1)
    sub = lax.broadcasted_iota(jnp.int32, (8, K), 0)
    tiles = list(tiles)
    cols = [lane_broadcast(tiles[0], k) for k in range(8)]
    for b in range(len(tiles)):
        cur = tiles[b]
        inside = (lane >= 8 * b) & (lane < 8 * b + 8)
        low = {(i, k): row_broadcast(cols[k], i) for k in range(8) for i in range(k, 8)}
        rows = [
            jnp.where(inside, jnp.where(lane == 8 * b + i, 1.0, 0.0), row_broadcast(cur, i))
            for i in range(8)
        ]
        inv = [None] * 8
        for k in range(0, 8, 2):
            p, q, r = low[k, k], low[k + 1, k], low[k + 1, k + 1]
            inv[k] = lax.rsqrt(p)
            inv[k + 1] = (p * inv[k]) * lax.rsqrt(p * r - q * q)
            low[k + 1, k] = q * inv[k]
            for i in range(k + 2, 8):
                low[i, k] = low[i, k] * inv[k]
                low[i, k + 1] = (low[i, k + 1] - low[i, k] * low[k + 1, k]) * inv[k + 1]
            for i in range(k + 2, 8):
                for m in range(k + 2, i + 1):
                    low[i, m] = (low[i, m] - low[i, k] * low[m, k]) - low[i, k + 1] * low[m, k + 1]
        for k in range(8):
            rows[k] = rows[k] * inv[k]
            for i in range(k + 1, 8):
                rows[i] = rows[i] - low[i, k] * rows[k]
        for t in range(b + 1, len(tiles)):
            col = [lane_broadcast(tiles[t], 8 * b + k) for k in range(8)]
            ahead = [lane_broadcast(tiles[t], 8 * t + k) for k in range(8)] if t == b + 1 else []
            acc = jnp.where(inside, 0.0, tiles[t])
            for k in range(8):
                col[k] = col[k] * inv[k]
                for m in range(k + 1, 8):
                    col[m] = col[m] - col[k] * low[m, k]
                acc = acc - col[k] * rows[k]
            tiles[t] = acc
            if ahead:
                for m in range(8):
                    ahead = [a - col[m] * row_broadcast(col[m], k) for k, a in enumerate(ahead)]
                cols = ahead
        new = rows[0]
        for i in range(1, 8):
            new = jnp.where(sub == i, rows[i], new)
        tiles[b] = jnp.where(lane <= sub + 8 * b, new, 0.0)
    return tiles


def product(value, right_high, right_low):
    high, low = split(value)
    return dot(high, right_high) + (dot(high, right_low) + dot(low, right_high))


def kernel(
    x_hbm, s_hbm, basis_ref, column_ref, first_ref,
    x_in, s_in, x_high, x_low, s_pair, total, wide, tall,
    zfull,
    core_out, core_in, own, half, in1, part2, in2,
    gram, gram_in, gram_mid, gram_core, gram_z, gram_all, inverse,
    load_sem, core_send, core_recv, s1, r1, s2, r2,
    az_s, az_r, a1_s, a1_r, ac_s, ac_r,
    gx_s, gx_r, gc_s, gc_r, gz_s, gz_r, ga_s, ga_r,
):
    grp, row = lax.axis_index("grp"), lax.axis_index("row")
    x, core = grp // 2, grp % 2
    z, y = row // NY, row % NY
    other = 1 - core
    swap = core == 1
    first = jnp.where(swap, y, x)
    second = jnp.where(swap, x, y)

    def turn(at, step, size):
        return lax.rem(at + step, size)

    def device(px, pc, pz, py):
        return (px * 2 + pc, pz * NY + py)

    def by_axes(at_first, at_second, at_z):
        return device(jnp.where(swap, at_second, at_first), core, at_z, jnp.where(swap, at_first, at_second))

    near = (2, 1, 3)
    far_first = near + (0,)
    ring = (4, 3, 5, 2, 6, 1, 7)
    plane = [(i, j) for i in (2, 1, 3, 0) for j in (2, 1, 3, 0) if i or j]

    def in_plane(step):
        px, py = turn(x, step[0], NX), turn(y, step[1], NY)
        return px * 4 + py, device(px, core, z, py)

    partner = device(x, other, z, y)

    def remote(src, dst, send, recv, to):
        return pltpu.make_async_remote_copy(
            src_ref=src, dst_ref=dst, send_sem=send, recv_sem=recv, device_id=to, device_id_type=MESH
        )

    def arrived(ref, recv):
        remote(ref, ref, recv, recv, partner).wait_recv()

    def sent(ref, send):
        remote(ref, ref, send, send, partner).wait_send()

    loads = []
    for j in range(NBLOCK):
        cols = pl.ds(BLOCK * j, BLOCK)
        pair = (
            pltpu.make_async_copy(s_hbm.at[cols], s_in.at[j], load_sem.at[2 * j]),
            pltpu.make_async_copy(x_hbm.at[:, cols], x_in.at[j], load_sem.at[2 * j + 1]),
        )
        for copy in pair:
            copy.start()
        loads.append(pair)

    barrier = pltpu.get_barrier_semaphore()
    peers = [partner] + [in_plane(s)[1] for s in plane]
    peers += [by_axes(first, turn(second, i, 4), turn(z, k, NZ)) for i in range(4) for k in ring]
    for peer in peers:
        pl.semaphore_signal(barrier, inc=1, device_id=peer, device_id_type=MESH)

    def gram_start(g, block):
        product = jnp.dot(block.T, block, precision=HIGHEST, preferred_element_type=F32)
        gram[g] = product.reshape(16, 8, K)
        for k, s in enumerate(plane):
            at, to = in_plane(s)
            remote(gram.at[g, at], gram_in.at[g, k], gx_s.at[g], gx_r.at[g], to).start()

    def gram_core_step(g):
        arrived(gram_in.at[g], gx_r.at[g])
        tile = gram[g, x * 4 + y]
        for k in range(len(plane)):
            tile = tile + gram_in[g, k]
        gram_mid[g] = tile
        remote(gram_mid.at[g], gram_core.at[g], gc_s.at[g], gc_r.at[g], partner).start()

    def gram_z_step(g):
        arrived(gram_core.at[g], gc_r.at[g])
        gram_z[g, z] = gram_mid[g] + gram_core[g]
        for k in ring:
            to = by_axes(first, second, turn(z, k, NZ))
            remote(gram_z.at[g, z], gram_z.at[g, z], gz_s.at[g], gz_r.at[g], to).start()

    def gram_back_step(g):
        arrived(gram_z.at[g, pl.ds(0, 7)], gz_r.at[g])
        tile = gram_z[g, 0]
        for k in range(1, NZ):
            tile = tile + gram_z[g, k]
        at = x * 4 + y
        gram_all[g, at] = tile
        for s in plane:
            remote(gram_all.at[g, at], gram_all.at[g, at], ga_s.at[g], ga_r.at[g], in_plane(s)[1]).start()

    def gram_arrived(g):
        arrived(gram_all.at[g, pl.ds(0, 15)], ga_r.at[g])

    def factor(g):
        tiles, across = unit_diagonal([gram_all[g, t] for t in range(16)])
        tiles = eliminate(tiles)
        whole = jnp.concatenate([tile * across for tile in tiles], axis=0)
        high, low = split(whole.T)
        inverse[g, 0] = high
        inverse[g, 1] = low

    def normalized(value, g):
        return product(value, inverse[g, 0], inverse[g, 1])

    def transposed_block(j):
        part = dot(wide[...], x_high[j])
        part = part[0:K] + part[K : 2 * K] + dot(wide[0:K, :], x_low[j])
        return part.T.reshape(NZ, NY, SLAB, K)

    def prepare(block):
        high, low = split(block.T)
        wide[0:K, :] = high
        wide[K : 2 * K, :] = low

    def core_step(n):
        for i, step in enumerate(far_first):
            core_out[n, i] = transposed_block(turn(x, step, NX) * 2 + other)
            remote(core_out.at[n, i], core_in.at[n, i], core_send.at[n, i], core_recv.at[n, i], partner).start()

    def first_step(n):
        for k, step in enumerate(far_first):
            own[k] = transposed_block(turn(x, step, NX) * 2 + core)
        for k in range(NX):
            arrived(core_in.at[n, k], core_recv.at[n, k])
        for i in range(4):
            for k, step in enumerate(far_first):
                xi = jnp.where(swap, i, k)
                py = turn(y, jnp.where(swap, step, far_first[i]), NY)
                half[n, i, k] = own[xi, :, py] + core_in[n, xi, :, py]
                if step:
                    to = by_axes(turn(first, step, 4), second, z)
                    remote(half.at[n, i, k], in1.at[n, i, k], s1.at[n], r1.at[n, i], to).start()

    def second_step(n, i):
        arrived(in1.at[n, i], r1.at[n, i])
        part2[n, i] = (half[n, i, 3] + in1[n, i, 0]) + (in1[n, i, 1] + in1[n, i, 2])
        at_second = turn(second, far_first[i], 4)
        for k, step in enumerate(ring + (0,) if i < 3 else ring):
            at = turn(z, step, NZ)
            to = by_axes(first, at_second, at)
            remote(part2.at[n, i, at], in2.at[n, i * 8 + k], s2.at[n], r2.at[n], to).start()

    def slab_of(n):
        arrived(in2.at[n], r2.at[n])
        sums = [part2[n, 3, z]] + [in2[n, k] for k in range(31)]
        while len(sums) > 1:
            sums = [p + q for p, q in zip(sums[0::2], sums[1::2])]
        return sums[0]

    total[...] = jnp.zeros_like(total)
    for j in range(NBLOCK):
        for copy in loads[j]:
            copy.wait()
        s_high, s_low = split(s_in[j])
        s_pair[j, :, 0:K] = s_high
        s_pair[j, :, K : 2 * K] = s_low
        high, low = split(x_in[j])
        x_high[j] = high
        x_low[j] = low
        part = dot(high, s_pair[j])
        total[...] += part[:, 0:K] + part[:, K : 2 * K] + dot(low, s_high)
    image = total[...]
    prepare(image)
    pl.semaphore_wait(barrier, len(peers))

    gram_start(0, image)
    core_step(0)
    first_step(0)
    gram_core_step(0)
    gram_z_step(0)
    second_step(0, 0)
    second_step(0, 1)
    gram_back_step(0)
    second_step(0, 2)
    second_step(0, 3)
    slab = slab_of(0)

    zfull[core, first, second, z] = slab
    for away in (0, 1, 3, 2):
        for step in ring + (0,) if away else ring:
            to = by_axes(first, turn(second, away, 4), turn(z, step, NZ))
            mine = zfull.at[core, first, second, z]
            remote(mine, mine, az_s.at[0], az_r.at[away], to).start()
    for away in (0, 1, 3, 2):
        at_second = turn(second, 4 - away, 4)
        block = zfull.at[core, first, at_second]
        arrived(block if away else zfull.at[core, first, at_second, pl.ds(0, 7)], az_r.at[away])
        for step in near:
            to = by_axes(turn(first, step, 4), second, z)
            remote(block, block, a1_s.at[0], a1_r.at[away], to).start()
    gram_arrived(0)
    factor(0)
    for away in (0, 1, 3, 2):
        block = zfull.at[core, :, turn(second, 4 - away, 4)]
        arrived(zfull.at[core, pl.ds(0, 3), 0], a1_r.at[away])
        remote(block, block, ac_s.at[0], ac_r.at[0], partner).start()
    root_rows = math.sqrt(x_hbm.shape[0] * 256)

    def image_of(half_core, px):
        for py in range(NY):
            at_first = jnp.where(half_core == 1, py, px)
            at_second = jnp.where(half_core == 1, px, py)
            high, low = split(zfull[half_core, at_first, at_second])
            tall[px, :, py, :, 0:K] = high
            tall[px, :, py, :, K : 2 * K] = low
        right = tall[px].reshape(BLOCK, 2 * K)
        part = dot(x_high[px * 2 + half_core], right)
        return part[:, 0:K] + part[:, K : 2 * K] + dot(x_low[px * 2 + half_core], right[:, 0:K])

    total[...] = image_of(core, 0)
    for px in range(1, NX):
        total[...] += image_of(core, px)
    arrived(zfull.at[other], ac_r.at[0])
    for px in range(NX):
        total[...] += image_of(other, px)
    total[...] = normalized(total[...], 0)
    image = total[...]

    gram_start(1, image)
    prepare(image)
    core_step(1)
    first_step(1)
    gram_core_step(1)
    gram_z_step(1)
    second_step(1, 0)
    second_step(1, 1)
    gram_back_step(1)
    second_step(1, 2)
    second_step(1, 3)
    first_ref[...] = normalized(slab, 0) / root_rows
    gram_arrived(1)
    factor(1)
    basis_ref[...] = normalized(total[...], 1) * root_rows
    column_ref[...] = normalized(slab_of(1), 1) / root_rows

    for n in range(2):
        for px in range(NX):
            sent(core_out.at[n, px], core_send.at[n, px])
        sent(in1.at[n], s1.at[n])
        sent(in2.at[n], s2.at[n])
        sent(gram_in.at[n], gx_s.at[n])
        sent(gram_mid.at[n], gc_s.at[n])
        sent(gram_z.at[n, pl.ds(0, 7)], gz_s.at[n])
        sent(gram_all.at[n, pl.ds(0, 15)], ga_s.at[n])
    sent(in2.at[0], az_s.at[0])
    sent(in1.at[0], a1_s.at[0])
    sent(zfull.at[core], ac_s.at[0])


def hand_over(a, b, c, a_out, b_out, c_out, sem):
    copies = [
        pltpu.make_async_copy(src, dst, sem.at[k])
        for k, (src, dst) in enumerate(((a, a_out), (b, b_out), (c, c_out)))
    ]
    for copy in copies:
        copy.start()
    for copy in copies:
        copy.wait()


def per_device(embeddings, sketch):
    rows = embeddings.shape[0]
    dma = pltpu.SemaphoreType.DMA
    vmem = pltpu.VMEM
    scratch = [
        vmem((NBLOCK, rows, BLOCK), F32),
        vmem((NBLOCK, BLOCK, K), F32),
        vmem((NBLOCK, rows, BLOCK), BF16),
        vmem((NBLOCK, rows, BLOCK), BF16),
        vmem((NBLOCK, BLOCK, 2 * K), BF16),
        vmem((rows, K), F32),
        vmem((2 * K, rows), BF16),
        vmem((NX, NZ, NY, SLAB, 2 * K), BF16),
        vmem((2, 4, 4, NZ, SLAB, K), F32),
        vmem((2, NX, NZ, NY, SLAB, K), F32),
        vmem((2, NX, NZ, NY, SLAB, K), F32),
        vmem((NX, NZ, NY, SLAB, K), F32),
        vmem((2, 4, 4, NZ, SLAB, K), F32),
        vmem((2, 4, 3, NZ, SLAB, K), F32),
        vmem((2, 4, NZ, SLAB, K), F32),
        vmem((2, 31, SLAB, K), F32),
        vmem((2, 16, 8, K), F32),
        vmem((2, 15, 8, K), F32),
        vmem((2, 8, K), F32),
        vmem((2, 8, K), F32),
        vmem((2, NZ, 8, K), F32),
        vmem((2, 16, 8, K), F32),
        vmem((2, 2, K, K), BF16),
        dma((2 * NBLOCK,)),
        dma((2, NX)), dma((2, NX)),
        dma((2,)), dma((2, 4)),
        dma((2,)), dma((2,)),
        dma((1,)), dma((4,)),
        dma((1,)), dma((4,)),
        dma((1,)), dma((1,)),
        dma((2,)), dma((2,)),
        dma((2,)), dma((2,)),
        dma((2,)), dma((2,)),
        dma((2,)), dma((2,)),
    ]
    results = pl.pallas_call(
        kernel,
        name="subspace_iteration",
        out_shape=(
            jax.ShapeDtypeStruct((rows, K), F32),
            jax.ShapeDtypeStruct((SLAB, K), F32),
            jax.ShapeDtypeStruct((SLAB, K), F32),
        ),
        in_specs=[pl.BlockSpec(memory_space=pltpu.HBM)] * 2,
        out_specs=[pl.BlockSpec(memory_space=pltpu.VMEM)] * 3,
        scratch_shapes=scratch,
        compiler_params=pltpu.CompilerParams(
            collective_id=0, has_side_effects=True, vmem_limit_bytes=52 * 2**20
        ),
        cost_estimate=pl.CostEstimate(
            flops=4 * 2 * rows * embeddings.shape[1] * K, bytes_accessed=11 * 2**20, transcendentals=0
        ),
    )(embeddings, sketch)
    return pl.pallas_call(
        hand_over,
        name="hand_over",
        out_shape=tuple(jax.ShapeDtypeStruct(r.shape, r.dtype) for r in results),
        in_specs=[pl.BlockSpec(memory_space=pl.ANY)] * 3,
        out_specs=[pl.BlockSpec(memory_space=pl.ANY)] * 3,
        scratch_shapes=[dma((3,))],
        compiler_params=pltpu.CompilerParams(vmem_limit_bytes=2**20),
    )(*results)


def solution(mesh):
    rows = P(("grp", "row"), None)
    return jax.shard_map(
        per_device, mesh=mesh, in_specs=(rows, P()), out_specs=(rows, rows, rows), check_vma=False
    )
```

```python
import math

import jax
import jax.numpy as jnp
from jax import lax
from jax.experimental import pallas as pl
from jax.experimental.pallas import tpu as pltpu
from jax.sharding import PartitionSpec as P

MESH = pl.DeviceIdType.MESH
HIGHEST = lax.Precision.HIGHEST
F32, BF16 = jnp.float32, jnp.bfloat16
K = 128
NX, NY, NZ = 4, 4, 8
SLAB = 16
BLOCK = NY * NZ * SLAB
NBLOCK = 2 * NX


def split(value):
    high = value.astype(BF16)
    return high, (value - high.astype(F32)).astype(BF16)


def dot(left, right):
    return jnp.dot(left, right, preferred_element_type=F32)


def lane_broadcast(value, lane):
    return jnp.broadcast_to(value[:, lane : lane + 1], value.shape)


def row_broadcast(value, row):
    return jnp.broadcast_to(value[row : row + 1, :], value.shape)


def tree_sum(terms):
    while len(terms) > 1:
        terms = [p + q for p, q in zip(terms[0::2], terms[1::2])]
    return terms[0]


def unit_diagonal(tiles):
    lane = lax.broadcasted_iota(jnp.int32, (8, K), 1)
    sub = lax.broadcasted_iota(jnp.int32, (8, K), 0)
    diagonal = [jnp.where(lane == sub + 8 * t, tile, 0.0) for t, tile in enumerate(tiles)]
    across = jnp.broadcast_to(lax.rsqrt(jnp.sum(tree_sum(diagonal), axis=0, keepdims=True)), (8, K))
    down = [lax.rsqrt(jnp.broadcast_to(jnp.sum(d, axis=1, keepdims=True), (8, K))) for d in diagonal]
    return [tile * d * across for tile, d in zip(tiles, down)], across


def eliminate(tiles):
    lane = lax.broadcasted_iota(jnp.int32, (8, K), 1)
    sub = lax.broadcasted_iota(jnp.int32, (8, K), 0)
    tiles = list(tiles)
    cols = [lane_broadcast(tiles[0], k) for k in range(8)]
    for b in range(len(tiles)):
        cur = tiles[b]
        inside = (lane >= 8 * b) & (lane < 8 * b + 8)
        low = {(i, k): row_broadcast(cols[k], i) for k in range(8) for i in range(k, 8)}
        rows = [
            jnp.where(inside, jnp.where(lane == 8 * b + i, 1.0, 0.0), row_broadcast(cur, i))
            for i in range(8)
        ]
        inv = [None] * 8
        for k in range(0, 8, 2):
            p, q, r = low[k, k], low[k + 1, k], low[k + 1, k + 1]
            inv[k] = lax.rsqrt(p)
            inv[k + 1] = (p * inv[k]) * lax.rsqrt(p * r - q * q)
            low[k + 1, k] = q * inv[k]
            for i in range(k + 2, 8):
                low[i, k] = low[i, k] * inv[k]
                low[i, k + 1] = (low[i, k + 1] - low[i, k] * low[k + 1, k]) * inv[k + 1]
            for i in range(k + 2, 8):
                for m in range(k + 2, i + 1):
                    low[i, m] = (low[i, m] - low[i, k] * low[m, k]) - low[i, k + 1] * low[m, k + 1]
        for k in range(8):
            rows[k] = rows[k] * inv[k]
            for i in range(k + 1, 8):
                rows[i] = rows[i] - low[i, k] * rows[k]
        for t in range(b + 1, len(tiles)):
            col = [lane_broadcast(tiles[t], 8 * b + k) for k in range(8)]
            ahead = [lane_broadcast(tiles[t], 8 * t + k) for k in range(8)] if t == b + 1 else []
            acc = jnp.where(inside, 0.0, tiles[t])
            for k in range(8):
                col[k] = col[k] * inv[k]
                for m in range(k + 1, 8):
                    col[m] = col[m] - col[k] * low[m, k]
                acc = acc - col[k] * rows[k]
            tiles[t] = acc
            if ahead:
                for m in range(8):
                    ahead = [a - col[m] * row_broadcast(col[m], k) for k, a in enumerate(ahead)]
                cols = ahead
        new = rows[0]
        for i in range(1, 8):
            new = jnp.where(sub == i, rows[i], new)
        tiles[b] = jnp.where(lane <= sub + 8 * b, new, 0.0)
    return tiles


def product(value, right_high, right_low):
    high, low = split(value)
    return dot(high, right_high) + (dot(high, right_low) + dot(low, right_high))


def kernel(
    x_hbm, s_hbm, basis_ref, column_ref, first_ref,
    x_in, s_in, x_high, x_low, s_pair, total, wide, tall,
    zfull,
    core_out, core_in, own, half, in1, part2, in2,
    gram, gram_in, gram_z, gram_all, inverse,
    load_sem, core_send, core_recv, s1, r1, s2, r2,
    az_s, az_r, a1_s, a1_r, ac_s, ac_r,
    gx_s, gx_r, gz_s, gz_r, ga_s, ga_r,
):
    grp, row = lax.axis_index("grp"), lax.axis_index("row")
    x, core = grp // 2, grp % 2
    z, y = row // NY, row % NY
    other = 1 - core
    swap = core == 1
    first = jnp.where(swap, y, x)
    second = jnp.where(swap, x, y)

    def turn(at, step, size):
        return lax.rem(at + step, size)

    def device(px, pc, pz, py):
        return (px * 2 + pc, pz * NY + py)

    def by_axes(at_first, at_second, at_z):
        return device(jnp.where(swap, at_second, at_first), core, at_z, jnp.where(swap, at_first, at_second))

    near = (2, 1, 3)
    far_first = near + (0,)
    ring = (4, 3, 5, 2, 6, 1, 7)
    plane = [(i, j) for i in (2, 1, 3, 0) for j in (2, 1, 3, 0) if i or j]

    def in_plane(step):
        px, py = turn(x, step[0], NX), turn(y, step[1], NY)
        return px * 4 + py, device(px, core, z, py)

    partner = device(x, other, z, y)
    column = [device(x, c, turn(z, k, NZ), y) for k in ring for c in (core, other)] + [partner]

    def remote(src, dst, send, recv, to):
        return pltpu.make_async_remote_copy(
            src_ref=src, dst_ref=dst, send_sem=send, recv_sem=recv, device_id=to, device_id_type=MESH
        )

    def arrived(ref, recv):
        remote(ref, ref, recv, recv, partner).wait_recv()

    def sent(ref, send):
        remote(ref, ref, send, send, partner).wait_send()

    loads = []
    for j in range(NBLOCK):
        cols = pl.ds(BLOCK * j, BLOCK)
        pair = (
            pltpu.make_async_copy(s_hbm.at[cols], s_in.at[j], load_sem.at[2 * j]),
            pltpu.make_async_copy(x_hbm.at[:, cols], x_in.at[j], load_sem.at[2 * j + 1]),
        )
        for copy in pair:
            copy.start()
        loads.append(pair)

    barrier = pltpu.get_barrier_semaphore()
    peers = [partner] + [in_plane(s)[1] for s in plane]
    peers += [by_axes(first, turn(second, i, 4), turn(z, k, NZ)) for i in range(4) for k in ring]
    peers += [device(x, other, turn(z, k, NZ), y) for k in ring]
    for peer in peers:
        pl.semaphore_signal(barrier, inc=1, device_id=peer, device_id_type=MESH)

    def gram_start(g, block):
        product = jnp.dot(block.T, block, precision=HIGHEST, preferred_element_type=F32)
        gram[g] = product.reshape(16, 8, K)
        for k, s in enumerate(plane):
            at, to = in_plane(s)
            remote(gram.at[g, at], gram_in.at[g, k], gx_s.at[g], gx_r.at[g], to).start()

    def gram_z_step(g):
        arrived(gram_in.at[g], gx_r.at[g])
        at = core * NZ + z
        gram_z[g, at] = tree_sum([gram[g, x * 4 + y]] + [gram_in[g, k] for k in range(15)])
        for to in column:
            remote(gram_z.at[g, at], gram_z.at[g, at], gz_s.at[g], gz_r.at[g], to).start()

    def gram_back_step(g):
        arrived(gram_z.at[g, pl.ds(0, 15)], gz_r.at[g])
        tile = tree_sum([gram_z[g, k] for k in range(16)])
        at = x * 4 + y
        gram_all[g, at] = tile
        for s in plane:
            remote(gram_all.at[g, at], gram_all.at[g, at], ga_s.at[g], ga_r.at[g], in_plane(s)[1]).start()

    def gram_arrived(g):
        arrived(gram_all.at[g, pl.ds(0, 15)], ga_r.at[g])

    def factor(g):
        tiles, across = unit_diagonal([gram_all[g, t] for t in range(16)])
        tiles = eliminate(tiles)
        whole = jnp.concatenate([tile * across for tile in tiles], axis=0)
        high, low = split(whole.T)
        inverse[g, 0] = high
        inverse[g, 1] = low

    def normalized(value, g):
        return product(value, inverse[g, 0], inverse[g, 1])

    def transposed_block(j):
        part = dot(wide[...], x_high[j])
        part = part[0:K] + part[K : 2 * K] + dot(wide[0:K, :], x_low[j])
        return part.T.reshape(NZ, NY, SLAB, K)

    def prepare(block):
        high, low = split(block.T)
        wide[0:K, :] = high
        wide[K : 2 * K, :] = low

    def core_step(n):
        for i, step in enumerate(far_first):
            core_out[n, i] = transposed_block(turn(x, step, NX) * 2 + other)
            remote(core_out.at[n, i], core_in.at[n, i], core_send.at[n, i], core_recv.at[n, i], partner).start()

    def first_step(n):
        for k, step in enumerate(far_first):
            own[k] = transposed_block(turn(x, step, NX) * 2 + core)
        for k in range(NX):
            arrived(core_in.at[n, k], core_recv.at[n, k])
        for i in range(4):
            for k, step in enumerate(far_first):
                xi = jnp.where(swap, i, k)
                py = turn(y, jnp.where(swap, step, far_first[i]), NY)
                half[n, i, k] = own[xi, :, py] + core_in[n, xi, :, py]
                if step:
                    to = by_axes(turn(first, step, 4), second, z)
                    remote(half.at[n, i, k], in1.at[n, i, k], s1.at[n], r1.at[n, i], to).start()

    def second_step(n, i):
        arrived(in1.at[n, i], r1.at[n, i])
        part2[n, i] = (half[n, i, 3] + in1[n, i, 0]) + (in1[n, i, 1] + in1[n, i, 2])
        at_second = turn(second, far_first[i], 4)
        for k, step in enumerate(ring + (0,) if i < 3 else ring):
            at = turn(z, step, NZ)
            to = by_axes(first, at_second, at)
            remote(part2.at[n, i, at], in2.at[n, i * 8 + k], s2.at[n], r2.at[n], to).start()

    def slab_of(n):
        arrived(in2.at[n], r2.at[n])
        return tree_sum([part2[n, 3, z]] + [in2[n, k] for k in range(31)])

    total[...] = jnp.zeros_like(total)
    for j in range(NBLOCK):
        for copy in loads[j]:
            copy.wait()
        s_high, s_low = split(s_in[j])
        s_pair[j, :, 0:K] = s_high
        s_pair[j, :, K : 2 * K] = s_low
        high, low = split(x_in[j])
        x_high[j] = high
        x_low[j] = low
        part = dot(high, s_pair[j])
        total[...] += part[:, 0:K] + part[:, K : 2 * K] + dot(low, s_high)
    image = total[...]
    prepare(image)
    pl.semaphore_wait(barrier, len(peers))

    gram_start(0, image)
    core_step(0)
    first_step(0)
    gram_z_step(0)
    second_step(0, 0)
    second_step(0, 1)
    gram_back_step(0)
    second_step(0, 2)
    second_step(0, 3)
    slab = slab_of(0)

    zfull[core, first, second, z] = slab
    for away in (0, 1, 3, 2):
        for step in ring + (0,) if away else ring:
            to = by_axes(first, turn(second, away, 4), turn(z, step, NZ))
            mine = zfull.at[core, first, second, z]
            remote(mine, mine, az_s.at[0], az_r.at[away], to).start()
    for away in (0, 1, 3, 2):
        at_second = turn(second, 4 - away, 4)
        block = zfull.at[core, first, at_second]
        arrived(block if away else zfull.at[core, first, at_second, pl.ds(0, 7)], az_r.at[away])
        for step in near:
            to = by_axes(turn(first, step, 4), second, z)
            remote(block, block, a1_s.at[0], a1_r.at[away], to).start()
    gram_arrived(0)
    factor(0)
    for away in (0, 1, 3, 2):
        block = zfull.at[core, :, turn(second, 4 - away, 4)]
        arrived(zfull.at[core, pl.ds(0, 3), 0], a1_r.at[away])
        remote(block, block, ac_s.at[0], ac_r.at[0], partner).start()
    root_rows = math.sqrt(x_hbm.shape[0] * 256)

    def image_of(half_core, px):
        for py in range(NY):
            at_first = jnp.where(half_core == 1, py, px)
            at_second = jnp.where(half_core == 1, px, py)
            high, low = split(zfull[half_core, at_first, at_second])
            tall[px, :, py, :, 0:K] = high
            tall[px, :, py, :, K : 2 * K] = low
        right = tall[px].reshape(BLOCK, 2 * K)
        part = dot(x_high[px * 2 + half_core], right)
        return part[:, 0:K] + part[:, K : 2 * K] + dot(x_low[px * 2 + half_core], right[:, 0:K])

    total[...] = image_of(core, 0)
    for px in range(1, NX):
        total[...] += image_of(core, px)
    arrived(zfull.at[other], ac_r.at[0])
    for px in range(NX):
        total[...] += image_of(other, px)
    total[...] = normalized(total[...], 0)
    image = total[...]

    gram_start(1, image)
    prepare(image)
    core_step(1)
    first_step(1)
    gram_z_step(1)
    second_step(1, 0)
    second_step(1, 1)
    gram_back_step(1)
    second_step(1, 2)
    second_step(1, 3)
    first_ref[...] = normalized(slab, 0) / root_rows
    gram_arrived(1)
    factor(1)
    basis_ref[...] = normalized(total[...], 1) * root_rows
    column_ref[...] = normalized(slab_of(1), 1) / root_rows

    for n in range(2):
        for px in range(NX):
            sent(core_out.at[n, px], core_send.at[n, px])
        sent(in1.at[n], s1.at[n])
        sent(in2.at[n], s2.at[n])
        sent(gram_in.at[n], gx_s.at[n])
        sent(gram_z.at[n, pl.ds(0, 15)], gz_s.at[n])
        sent(gram_all.at[n, pl.ds(0, 15)], ga_s.at[n])
    sent(in2.at[0], az_s.at[0])
    sent(in1.at[0], a1_s.at[0])
    sent(zfull.at[core], ac_s.at[0])


def hand_over(a, b, c, a_out, b_out, c_out, sem):
    copies = [
        pltpu.make_async_copy(src, dst, sem.at[k])
        for k, (src, dst) in enumerate(((a, a_out), (b, b_out), (c, c_out)))
    ]
    for copy in copies:
        copy.start()
    for copy in copies:
        copy.wait()


def per_device(embeddings, sketch):
    rows = embeddings.shape[0]
    dma = pltpu.SemaphoreType.DMA
    vmem = pltpu.VMEM
    scratch = [
        vmem((NBLOCK, rows, BLOCK), F32),
        vmem((NBLOCK, BLOCK, K), F32),
        vmem((NBLOCK, rows, BLOCK), BF16),
        vmem((NBLOCK, rows, BLOCK), BF16),
        vmem((NBLOCK, BLOCK, 2 * K), BF16),
        vmem((rows, K), F32),
        vmem((2 * K, rows), BF16),
        vmem((NX, NZ, NY, SLAB, 2 * K), BF16),
        vmem((2, 4, 4, NZ, SLAB, K), F32),
        vmem((2, NX, NZ, NY, SLAB, K), F32),
        vmem((2, NX, NZ, NY, SLAB, K), F32),
        vmem((NX, NZ, NY, SLAB, K), F32),
        vmem((2, 4, 4, NZ, SLAB, K), F32),
        vmem((2, 4, 3, NZ, SLAB, K), F32),
        vmem((2, 4, NZ, SLAB, K), F32),
        vmem((2, 31, SLAB, K), F32),
        vmem((2, 16, 8, K), F32),
        vmem((2, 15, 8, K), F32),
        vmem((2, 2 * NZ, 8, K), F32),
        vmem((2, 16, 8, K), F32),
        vmem((2, 2, K, K), BF16),
        dma((2 * NBLOCK,)),
        dma((2, NX)), dma((2, NX)),
        dma((2,)), dma((2, 4)),
        dma((2,)), dma((2,)),
        dma((1,)), dma((4,)),
        dma((1,)), dma((4,)),
        dma((1,)), dma((1,)),
        dma((2,)), dma((2,)),
        dma((2,)), dma((2,)),
        dma((2,)), dma((2,)),
    ]
    results = pl.pallas_call(
        kernel,
        name="subspace_iteration",
        out_shape=(
            jax.ShapeDtypeStruct((rows, K), F32),
            jax.ShapeDtypeStruct((SLAB, K), F32),
            jax.ShapeDtypeStruct((SLAB, K), F32),
        ),
        in_specs=[pl.BlockSpec(memory_space=pltpu.HBM)] * 2,
        out_specs=[pl.BlockSpec(memory_space=pltpu.VMEM)] * 3,
        scratch_shapes=scratch,
        compiler_params=pltpu.CompilerParams(
            collective_id=0, has_side_effects=True, vmem_limit_bytes=52 * 2**20
        ),
        cost_estimate=pl.CostEstimate(
            flops=4 * 2 * rows * embeddings.shape[1] * K, bytes_accessed=11 * 2**20, transcendentals=0
        ),
    )(embeddings, sketch)
    return pl.pallas_call(
        hand_over,
        name="hand_over",
        out_shape=tuple(jax.ShapeDtypeStruct(r.shape, r.dtype) for r in results),
        in_specs=[pl.BlockSpec(memory_space=pl.ANY)] * 3,
        out_specs=[pl.BlockSpec(memory_space=pl.ANY)] * 3,
        scratch_shapes=[dma((3,))],
        compiler_params=pltpu.CompilerParams(vmem_limit_bytes=2**20),
    )(*results)


def solution(mesh):
    rows = P(("grp", "row"), None)
    return jax.shard_map(
        per_device, mesh=mesh, in_specs=(rows, P()), out_specs=(rows, rows, rows), check_vma=False
    )
```
